32 devices in a mesh: dp: 4 (over x, core), tensor: 8 (over z, y).
Axes of the slice: x: 2, y: 2, z: 4, core: 2. Of those that a mesh axis runs over, the one named last changes fastest.
Arguments:
- tokens: bfloat16 [4, 128, 2048], P('dp'), may hold values from -6 to 6
- segments: int32 [4, 128], P('dp'), may hold values from 0 to 3, never falling along the last dimension, each value on 1 to 64 neighbouring positions
- cotangent: bfloat16 [4, 128, 2048], P('dp'), may hold values from -6 to 6
- mixer_input_weight: bfloat16 [2048, 2, 4096], P(None, None, 'tensor'), may hold values from -0.125 to 0.125
- conv_w: float32 [4096, 4], P('tensor'), may hold values from -3 to 3
- conv_b: float32 [4096], P('tensor'), may hold values from -0.5 to 0.5
- w_state: bfloat16 [4096, 160], P('tensor'), may hold values from -0.09375 to 0.09375
- w_step: bfloat16 [128, 4096], P(None, 'tensor'), may hold values from -0.5 to 0.5
- dt_bias: float32 [4096], P('tensor'), may hold values from -6.9 to -2.3
- a_log: float32 [4096, 16], P('tensor'), may hold values from 0 to 2.77
- d_skip: float32 [4096], P('tensor'), may hold values from 0.5 to 1.5
- w_mix_out: bfloat16 [4096, 2048], P('tensor'), may hold values from -0.09375 to 0.09375
- w_gate_up_early: bfloat16 [2048, 2, 8192], P(None, None, 'tensor'), may hold values from -0.125 to 0.125
- w_down_early: bfloat16 [8192, 2048], P('tensor'), may hold values from -0.0625 to 0.0625
- w_qkv: bfloat16 [2048, 3, 2048], P(None, None, 'tensor'), may hold values from -0.125 to 0.125
- w_attn_out: bfloat16 [2048, 2048], P('tensor'), may hold values from -0.5 to 0.5
- w_gate_up: bfloat16 [2048, 2, 8192], P(None, None, 'tensor'), may hold values from -0.125 to 0.125
- w_down: bfloat16 [8192, 2048], P('tensor'), may hold values from -0.0625 to 0.0625
- gain_one: float32 [2048], replicated, may hold values from 0.5 to 1.5
- gain_two: float32 [2048], replicated, may hold values from 0.5 to 1.5
- gain_three: float32 [2048], replicated, may hold values from 0.5 to 1.5
- gain_four: float32 [2048], replicated, may hold values from 0.5 to 1.5
Outputs:
- mixed: bfloat16 [4, 128, 2048], P('dp', 'tensor')
- tokens_grad: bfloat16 [4, 128, 2048], P('dp', 'tensor')
- grad_w_mix: float32 [2048, 2, 4096], P('dp', None, 'tensor')
- grad_conv_w: float32 [4096, 4], P(('tensor', 'dp'))
- grad_conv_b: float32 [4096], P(('tensor', 'dp'))
- grad_w_state: float32 [4096, 160], P(('tensor', 'dp'))
- grad_w_step: float32 [128, 4096], P('dp', 'tensor')
- grad_dt_bias: float32 [4096], P(('tensor', 'dp'))
- grad_a_log: float32 [4096, 16], P(('tensor', 'dp'))
- grad_d_skip: float32 [4096], P(('tensor', 'dp'))
- grad_w_mix_out: float32 [4096, 2048], P(('tensor', 'dp'))
- grad_w_gate_up_early: float32 [2048, 2, 8192], P('dp', None, 'tensor')
- grad_w_down_early: float32 [8192, 2048], P(('tensor', 'dp'))
- grad_w_qkv: float32 [2048, 3, 2048], P('dp', None, 'tensor')
- grad_w_attn_out: float32 [2048, 2048], P(('tensor', 'dp'))
- grad_w_gate_up: float32 [2048, 2, 8192], P('dp', None, 'tensor')
- grad_w_down: float32 [8192, 2048], P(('tensor', 'dp'))
- grad_gain_one: float32 [2048], replicated
- grad_gain_two: float32 [2048], P('dp')
- grad_gain_three: float32 [2048], P('dp')
- grad_gain_four: float32 [2048], P('dp')
The draws below stay inside these ranges and needn't reach their ends.
Inputs may be any that keep to these rules, and one draw needn't show every extreme that they name: `segments`: within a row segment numbers never fall; a row holds 4 documents, each of at most 64 tokens.
All inputs are finite; a program needn't handle non-finite values.
Results may differ from the reference program's by a relative error of at most 0.03.
Values sent between devices are 32-bit elements; how exact they have to be, the bound alone decides.
A program may use at most 320 MiB of HBM per device.

```python
import math
import jax
import jax.numpy as jnp
import numpy as np
from jax import lax

D = 2048
E = 4096
STATE = 16
RANK = 128
CONV = 4
FF = 8192
HEADS = 16
HEAD = 128
WINDOW = 2048
SEGS = 4
TOK_DEV = 128
ROWS = 4
QW = 2048


def steps_of(key, dims, pieces, smallest, top_value):
    def one(axis_at, shards_of):
        heights = jax.random.uniform(jax.random.fold_in(jax.random.fold_in(key, 6), axis_at), (shards_of,), jnp.float32, smallest / len(pieces), top_value / len(pieces))
        return jnp.repeat(jnp.exp(heights), dims[axis_at] // shards_of).reshape((-1,) + (1,) * (len(dims) - axis_at - 1))

    factor_of = one(*pieces[0])
    for cut in pieces[1:]:
        factor_of = factor_of * one(*cut)
    return factor_of


def split_up(amount, total, reach, slope):
    loads = [(1 << 20) // math.isqrt(grade ** slope) + 1 for grade in range(2, amount + 1)]
    surplus, given = total - reach - (amount - 1), [1] * (amount - 1)
    while surplus > 0:
        candidates = [i for i in range(amount - 1) if given[i] < reach]
        mass, left = sum([loads[i] for i in candidates]), surplus
        for i in candidates:
            extra = min(reach - given[i], max(1, left * loads[i] // mass), surplus)
            given[i] = given[i] + extra
            surplus = surplus - extra
    return np.array([reach] + given)


def ragged(stream_key, amount, total, limit, slope):
    if amount == 2:
        one = jax.random.randint(stream_key, (), max(1, total - limit), min(limit, total - 1) + 1)
        return jnp.stack([one, total - one])
    lengths = jnp.asarray(split_up(amount, total, limit, slope), jnp.int32)
    couples = (amount - 1) // 2
    donor, taker = lengths[1:1 + 2 * couples:2], lengths[2:2 + 2 * couples:2]
    slack = jnp.minimum(donor - 1, limit - taker)
    moved = jax.random.randint(jax.random.fold_in(stream_key, 1), (couples,), 0, 1 << 20) % (slack + 1)
    lengths = lengths.at[1:1 + 2 * couples:2].set(donor - moved).at[2:2 + 2 * couples:2].set(taker + moved)
    return lengths[jax.random.permutation(jax.random.fold_in(stream_key, 2), amount)]


def bell_draw(key, dims, deviation, bound, shards=(), held_as=jnp.bfloat16):
    array = jax.random.normal(key, dims, jnp.float32) * deviation
    if len(shards) > 0:
        array = steps_of(key, dims, shards, -0.22, 0.18) * array
    return jnp.clip(array, min=-bound, max=bound).astype(held_as)


def setup_inputs(seed: int = 0) -> dict:
    keys = jax.random.split(jax.random.key(seed), 23)
    tokens = bell_draw(keys[0], (ROWS, TOK_DEV, D), 1.0, 6.0, ((0, 4),))
    segments = jax.vmap(lambda own: jnp.searchsorted(jnp.cumsum(ragged(own, SEGS, TOK_DEV, TOK_DEV // 2, 0)), jnp.arange(TOK_DEV), side="right"))(jax.random.split(keys[1], ROWS)).reshape((ROWS, TOK_DEV)).astype(jnp.int32)
    cotangent = bell_draw(keys[2], (ROWS, TOK_DEV, D), 1.0, 6.0, ((0, 4),))
    mixer_input_weight = bell_draw(keys[3], (D, 2, E), D ** -0.5, 0.125, ((2, 8),))
    conv_w = bell_draw(keys[4], (E, CONV), CONV ** -0.5, 3.0, ((0, 8),), jnp.float32)
    conv_b = jnp.clip(jax.random.uniform(keys[5], (E,), jnp.float32, -0.5, 0.5) * steps_of(keys[5], (E,), ((0, 8),), -0.4, 0.0), -0.5, 0.5)
    w_state = bell_draw(keys[6], (E, RANK + 2 * STATE), E ** -0.5, 0.09375, ((0, 8),))
    w_step = bell_draw(keys[7], (RANK, E), RANK ** -0.5, 0.5, ((1, 8),))
    dt_bias = jnp.clip(-6.9 + 4.6000001430511475 * jax.random.uniform(keys[8], (E,), jnp.float32) ** steps_of(keys[8], (E,), ((0, 8),), -0.2, 0.2), -6.9, -2.3)
    a_log = jnp.clip(2.77 * jax.random.uniform(keys[9], (E, STATE), jnp.float32) ** steps_of(keys[9], (E, STATE), ((0, 8),), -0.2, 0.2), 0.0, 2.77)
    d_skip = jnp.clip(0.5 + 1.0 * jax.random.uniform(keys[10], (E,), jnp.float32) ** steps_of(keys[10], (E,), ((0, 8),), -0.2, 0.2), 0.5, 1.5)
    w_mix_out = bell_draw(keys[11], (E, D), E ** -0.5, 0.09375, ((0, 8),))
    w_gate_up_early = bell_draw(keys[12], (D, 2, FF), D ** -0.5, 0.125, ((2, 8),))
    w_down_early = bell_draw(keys[13], (FF, D), FF ** -0.5, 0.0625, ((0, 8),))
    w_qkv = bell_draw(keys[14], (D, 3, QW), D ** -0.5, 0.125, ((2, 8),))
    w_attn_out = bell_draw(keys[15], (QW, D), (QW // 16) ** -0.5, 0.5, ((0, 8),))
    w_gate_up = bell_draw(keys[16], (D, 2, FF), D ** -0.5, 0.125, ((2, 8),))
    w_down = bell_draw(keys[17], (FF, D), FF ** -0.5, 0.0625, ((0, 8),))
    gain_one = jnp.clip(1.0 + 0.1 * jax.random.normal(keys[18], (D,), jnp.float32), 0.5, 1.5)
    gain_two = jnp.clip(1.0 + 0.1 * jax.random.normal(keys[19], (D,), jnp.float32), 0.5, 1.5)
    gain_three = jnp.clip(1.0 + 0.1 * jax.random.normal(keys[20], (D,), jnp.float32), 0.5, 1.5)
    gain_four = jnp.clip(1.0 + 0.1 * jax.random.normal(keys[21], (D,), jnp.float32), 0.5, 1.5)
    return {"tokens": tokens, "segments": segments, "cotangent": cotangent, "mixer_input_weight": mixer_input_weight, "conv_w": conv_w, "conv_b": conv_b, "w_state": w_state, "w_step": w_step, "dt_bias": dt_bias, "a_log": a_log, "d_skip": d_skip, "w_mix_out": w_mix_out, "w_gate_up_early": w_gate_up_early, "w_down_early": w_down_early, "w_qkv": w_qkv, "w_attn_out": w_attn_out, "w_gate_up": w_gate_up, "w_down": w_down, "gain_one": gain_one, "gain_two": gain_two, "gain_three": gain_three, "gain_four": gain_four}


EPSILON = 1e-05
EXACT_MATMUL = lax.Precision.HIGHEST

@jax.custom_vjp
def low(v):
    return lax.optimization_barrier(v.astype(jnp.bfloat16)).astype(jnp.float32)

@jax.custom_vjp
def low_back(v):
    return v

def low_keep(v):
    return (low(v), None)

def low_pass(kept, grad):
    return (grad,)

def back_keep(v):
    return (v, None)

def back_low(kept, grad):
    return (low(grad),)
low.defvjp(low_keep, low_pass)
low_back.defvjp(back_keep, back_low)

def rms_norm(values, gain_vec):
    return values * lax.rsqrt(lax.optimization_barrier(jnp.mean(values * values, axis=-1, keepdims=True)) + EPSILON) * gain_vec

def product(left, right):
    return jnp.dot(left, right, precision=EXACT_MATMUL, preferred_element_type=jnp.float32)

def causal_conv(conv_in, doc_ids, conv_w, conv_b):
    width = conv_w.shape[1]
    running = conv_b[None, :] + conv_w[:, width - 1][None, :] * conv_in
    for offset in range(1, width):
        shifted = jnp.concatenate([jnp.zeros((offset, conv_in.shape[1]), conv_in.dtype), conv_in[:-offset]], axis=0)
        earlier_ids = jnp.concatenate([jnp.full((offset,), -1, jnp.int32), doc_ids[:-offset]])
        same_doc = jnp.where(earlier_ids == doc_ids, 1.0, 0.0).astype(conv_in.dtype)
        running = running + conv_w[:, width - 1 - offset][None, :] * shifted * same_doc[:, None]
    return jax.nn.silu(running)

def combine(earlier, later):
    return (earlier[0] * later[0], later[0] * earlier[1] + later[1])

def selective_scan(conv_act, step_pre, b_coef, c_coef, gate_z, dt_bias, a_log, d_skip, carry_mask):
    step_size = jax.nn.softplus(step_pre + dt_bias)
    rates = -jnp.exp(a_log)
    decays = jnp.exp(step_size[:, :, None] * rates[None]) * carry_mask[:, None, None]
    driving = (step_size * conv_act)[:, :, None] * b_coef[:, None, :]
    unused, states = lax.associative_scan(combine, (decays, driving), axis=0)
    result = jnp.einsum('ten,tn->te', states, c_coef, precision=EXACT_MATMUL) + d_skip * conv_act
    return result * jax.nn.silu(gate_z)

def doc_masks(doc_ids, float_type):
    seq_len = doc_ids.shape[0]
    fresh = jnp.concatenate([jnp.ones((1,), jnp.bool_), doc_ids[1:] != doc_ids[:-1]])
    carry_mask = jnp.where(fresh, 0.0, 1.0).astype(float_type)
    places = jnp.arange(seq_len, dtype=jnp.int32)
    apart = places[:, None] - places[None, :]
    allowed = (apart >= 0) & (apart < WINDOW) & (doc_ids[:, None] == doc_ids[None, :])
    return (carry_mask, allowed)

def swiglu_branch(resid, gain_vec, gate_up_weight, down_weight):
    normed = low(rms_norm(resid, gain_vec))
    gate_up = low_back(jnp.einsum('td,dsf->tsf', normed, gate_up_weight, precision=EXACT_MATMUL))
    hidden = low(jax.nn.silu(gate_up[:, 0]) * gate_up[:, 1])
    return resid + low_back(product(hidden, down_weight))

def block(resid_in, doc_ids, mixer_input_weight, conv_w, conv_b, w_state, w_step, dt_bias, a_log, d_skip, w_mix_out, w_gate_up_early, w_down_early, w_qkv, w_attn_out, w_gate_up, w_down, gain_one, gain_two, gain_three, gain_four):
    seq_len = resid_in.shape[0]
    carry_mask, allowed = doc_masks(doc_ids, resid_in.dtype)
    first_normalized_input = low(rms_norm(resid_in, gain_one))
    mixer_input_projected = low_back(jnp.einsum('oc,cyb->oyb', first_normalized_input, mixer_input_weight, precision=EXACT_MATMUL))
    conv_act = low(causal_conv(mixer_input_projected[:, 0], doc_ids, conv_w, conv_b))
    state_proj = product(conv_act, w_state)
    step_low = low(state_proj[:, :RANK])
    b_coef = state_proj[:, RANK:RANK + STATE]
    c_coef = state_proj[:, RANK + STATE:]
    step_pre = low_back(product(step_low, w_step))
    mixer_out = low(selective_scan(conv_act, step_pre, b_coef, c_coef, mixer_input_projected[:, 1], dt_bias, a_log, d_skip, carry_mask))
    resid_one = resid_in + low_back(product(mixer_out, w_mix_out))
    resid_two = swiglu_branch(resid_one, gain_two, w_gate_up_early, w_down_early)
    normed_three = low(rms_norm(resid_two, gain_three))
    qkv_all = low(low_back(jnp.einsum('td,dsq->tsq', normed_three, w_qkv, precision=EXACT_MATMUL)))
    queries = qkv_all[:, 0].reshape(seq_len, HEADS, HEAD)
    keys_all = qkv_all[:, 1].reshape(seq_len, HEADS, HEAD)
    values_all = qkv_all[:, 2].reshape(seq_len, HEADS, HEAD)
    scores = low_back(jnp.einsum('thd,shd->hts', queries, keys_all, precision=EXACT_MATMUL) * HEAD ** (-0.5))
    masked = jnp.where(allowed[None], scores, -1000000000.0)
    soft_low = low(jax.nn.softmax(masked, axis=-1))
    attended = low(low_back(jnp.einsum('hts,shd->thd', soft_low, values_all, precision=EXACT_MATMUL))).reshape(seq_len, QW)
    resid_three = resid_two + low_back(product(attended, w_attn_out))
    return swiglu_branch(resid_three, gain_four, w_gate_up, w_down)

def reference(tokens, segments, cotangent, mixer_input_weight, conv_w, conv_b, w_state, w_step, dt_bias, a_log, d_skip, w_mix_out, w_gate_up_early, w_down_early, w_qkv, w_attn_out, w_gate_up, w_down, gain_one, gain_two, gain_three, gain_four):
    params = (mixer_input_weight, conv_w, conv_b, w_state, w_step, dt_bias, a_log, d_skip, w_mix_out, w_gate_up_early, w_down_early, w_qkv, w_attn_out, w_gate_up, w_down, gain_one, gain_two, gain_three, gain_four)
    params = tuple((item.astype(jnp.float32) for item in params))

    def one_row(totals, row_data):
        row_in, row_ids, row_cot = row_data

        def forward(resid_in, *weights):
            return block(resid_in, row_ids, *weights)
        result, pullback = jax.vjp(forward, row_in.astype(jnp.float32), *params)
        grads = pullback(row_cot.astype(jnp.float32))
        totals = tuple((running + one_grad for running, one_grad in zip(totals, grads[1:])))
        return (totals, (result.astype(jnp.bfloat16), grads[0].astype(jnp.bfloat16)))
    zero_grads = tuple((jnp.zeros(item.shape, jnp.float32) for item in params))
    summed, outputs = lax.scan(one_row, zero_grads, (tokens, segments, cotangent))
    mixed, tokens_grad = outputs
    return (mixed, tokens_grad, summed[0], summed[1], summed[2], summed[3], summed[4], summed[5], summed[6], summed[7], summed[8], summed[9], summed[10], summed[11], summed[12], summed[13], summed[14], summed[15], summed[16], summed[17], summed[18])
```

```python
import functools

import jax
import jax.numpy as jnp
from jax import lax
from jax.experimental import pallas as pl
from jax.experimental.pallas import tpu as pltpu
from jax.sharding import PartitionSpec as P

HEAD = 128
WINDOW = 2048


EPSILON = 1e-05
EXACT_MATMUL = lax.Precision.HIGHEST


def rms_norm(values, gain_vec):
    return (
        values * lax.rsqrt(jnp.mean(values * values, axis=-1, keepdims=True) + EPSILON) * gain_vec
    )


def causal_conv(conv_in, doc_ids, conv_w, conv_b):
    width = conv_w.shape[1]
    running = conv_b[None, :] + conv_w[:, width - 1][None, :] * conv_in
    for offset in range(1, width):
        shifted = jnp.concatenate(
            [jnp.zeros((offset, conv_in.shape[1]), conv_in.dtype), conv_in[:-offset]], axis=0
        )
        earlier_ids = jnp.concatenate([jnp.full((offset,), -1, jnp.int32), doc_ids[:-offset]])
        same_doc = jnp.where(earlier_ids == doc_ids, 1.0, 0.0).astype(conv_in.dtype)
        running = running + conv_w[:, width - 1 - offset][None, :] * shifted * same_doc[:, None]
    return jax.nn.silu(running)


MESH = pl.DeviceIdType.MESH
DEPTH = 4
GROUP = 8


def remote(src, dst, send_sem, recv_sem, where):
    return pltpu.make_async_remote_copy(
        src_ref=src,
        dst_ref=dst,
        send_sem=send_sem,
        recv_sem=recv_sem,
        device_id=where,
        device_id_type=MESH,
    )


def exchange_kernel(sizes, plan, n_full, n_share, *refs):
    t_size, dp_size = sizes
    rows, lines = DEPTH, t_size // DEPTH
    half = dp_size // 2
    refs = list(refs)

    def take(count):
        return [refs.pop(0) for _ in range(count)]

    n_part = len(plan)
    parts, fulls, shares = take(n_part), take(n_full), take(n_share)
    outs, full_outs, share_outs = take(n_part), take(n_full), take(n_share)
    from_y, held, from_z = take(n_part), take(n_part), take(n_part)
    sy, ry, sz, rz, sgz, rgz, sgy, rgy = take(8)
    gather = n_full + n_share > 0
    if gather:
        local_sem, sdp, rdp = take(3)
    if n_full:
        srel, rrel = take(2)
    tensor, dp = lax.axis_index("tensor"), lax.axis_index("dp")
    z, y = tensor // lines, lax.rem(tensor, lines)
    x, core = dp // 2, lax.rem(dp, 2)
    across = [lax.rem(y + d, lines) for d in range(1, lines)]
    along = [lax.rem(z + d, rows) for d in range(1, rows)]
    others = [lax.rem(dp + d, dp_size) for d in range(1, dp_size)]
    twin = {"dp": x * 2 + 1 - core}

    def at_y(v):
        return {"tensor": z * lines + v}

    def at_z(v):
        return {"tensor": v * lines + y}

    barrier = pltpu.get_barrier_semaphore()
    greet = [at_y(v) for v in across] + [at_z(v) for v in along]
    if gather:
        greet += [{"dp": v} for v in others]
    for where in greet:
        pl.semaphore_signal(barrier, inc=1, device_id=where, device_id_type=MESH)
    pl.semaphore_wait(barrier, len(greet))

    steps = []
    for p, (scatter, chunks) in enumerate(plan):
        width = parts[p].shape[-1] // chunks
        for c in range(chunks):
            steps.append((p, scatter, slice(c * width, (c + 1) * width)))
    y_copies, z_copies, gz_copies, gy_copies = {}, {}, {}, {}
    for c, (p, scatter, col) in enumerate(steps):
        for d, v in enumerate(across):
            y_copies[c, d] = remote(
                parts[p].at[:, v, :, col],
                from_y[p].at[d, :, :, col],
                sy.at[c, d],
                ry.at[c, d],
                at_y(v),
            )
            y_copies[c, d].start()
    dp_copies, local_copies, x_full, relays = [], [], {}, []
    for i, (a, o) in enumerate(zip(fulls, full_outs)):
        local_copies.append(pltpu.make_async_copy(a, o.at[dp], local_sem.at[i]))
        local_copies[-1].start()
        for d in range(1, half):
            peer = lax.rem(x + d, half) * 2 + core
            x_full[i, d] = remote(
                a, o.at[dp], sdp.at[i, d - 1], rdp.at[i, d - 1], {"dp": peer}
            )
            x_full[i, d].start()
        dp_copies.append(
            remote(a, o.at[dp], sdp.at[i, half - 1], rdp.at[i, half - 1], twin)
        )
        dp_copies[-1].start()
    for i, (a, o) in enumerate(zip(shares, share_outs)):
        k = n_full + i
        local_copies.append(
            pltpu.make_async_copy(a.at[dp], o.at[dp], local_sem.at[k])
        )
        local_copies[-1].start()
        for d, peer in enumerate(others):
            dp_copies.append(
                remote(a.at[peer], o.at[dp], sdp.at[k, d], rdp.at[k, d], {"dp": peer})
            )
            dp_copies[-1].start()

    def step_y(c):
        p, scatter, col = steps[c]
        for d in range(lines - 1):
            y_copies[c, d].wait_recv()
        total = parts[p][:, y, :, col]
        for d in range(lines - 1):
            total = total + from_y[p][d, :, :, col]
        held[p][:, :, col] = total
        for d, v in enumerate(along):
            z_copies[c, d] = remote(
                held[p].at[v, :, col],
                from_z[p].at[d, :, col],
                sz.at[c, d],
                rz.at[c, d],
                at_z(v),
            )
            z_copies[c, d].start()

    def step_z(c):
        p, scatter, col = steps[c]
        for d in range(rows - 1):
            z_copies[c, d].wait_recv()
        total = held[p][z, :, col]
        for d in range(rows - 1):
            total = total + from_z[p][d, :, col]
        if scatter:
            outs[p][:, col] = total
            return
        outs[p][z, y, :, col] = total
        for d, v in enumerate(along):
            gz_copies[c, d] = remote(
                outs[p].at[z, y, :, col],
                outs[p].at[z, y, :, col],
                sgz.at[c, d],
                rgz.at[c, d],
                at_z(v),
            )
            gz_copies[c, d].start()

    def step_gz(c):
        p, scatter, col = steps[c]
        if scatter:
            return
        for d in range(rows - 1):
            gz_copies[c, d].wait_recv()
        for d, v in enumerate(across):
            gy_copies[c, d] = remote(
                outs[p].at[:, y, :, col],
                outs[p].at[:, y, :, col],
                sgy.at[c, d],
                rgy.at[c, d],
                at_y(v),
            )
            gy_copies[c, d].start()

    def step_gy(c):
        if steps[c][1]:
            return
        for d in range(lines - 1):
            gy_copies[c, d].wait_recv()

    stages = [step_y, step_z, step_gz, step_gy]
    for turn in range(len(steps) + len(stages) - 1):
        for lag in reversed(range(len(stages))):
            if 0 <= turn - lag < len(steps):
                stages[lag](turn - lag)
    for (i, d), copy in x_full.items():
        copy.wait_recv()
        source = lax.rem(x - d + half, half) * 2 + core
        row = full_outs[i].at[source]
        relays.append(remote(row, row, srel.at[i, d - 1], rrel.at[i, d - 1], twin))
        relays[-1].start()
    for group in (y_copies, z_copies, gz_copies, gy_copies, x_full):
        for copy in group.values():
            copy.wait_send()
    for copy in dp_copies + relays + local_copies:
        copy.wait()


def exchange(number, parts, fulls=(), shares=()):
    t_size, dp_size = lax.axis_size("tensor"), lax.axis_size("dp")
    rows, lines = DEPTH, t_size // DEPTH
    f32 = jnp.float32
    n_full, n_share = len(fulls), len(shares)
    vmem = pl.BlockSpec(memory_space=pltpu.VMEM)
    anywhere = pl.BlockSpec(memory_space=pl.ANY)
    dma = pltpu.SemaphoreType.DMA
    plan = tuple((scatter, chunks) for _, scatter, chunks in parts)
    total = sum(chunks for _, chunks in plan)
    share_rows = [a.shape[0] // t_size for a, _, _ in parts]
    widths = [a.shape[1] for a, _, _ in parts]
    pairs = list(zip(share_rows, widths))
    scratch = [pltpu.VMEM((lines - 1, rows, s, w), f32) for s, w in pairs]
    scratch += [pltpu.VMEM((rows, s, w), f32) for s, w in pairs]
    scratch += [pltpu.VMEM((rows - 1, s, w), f32) for s, w in pairs]
    for hops in (lines, lines, rows, rows, rows, rows, lines, lines):
        scratch.append(dma((total, hops - 1)))
    extra = n_full + n_share
    if extra:
        scratch += [dma((extra,)), dma((extra, dp_size - 1)), dma((extra, dp_size - 1))]
    if n_full:
        scratch += [dma((n_full, dp_size // 2 - 1))] * 2
    out_shape = [
        jax.ShapeDtypeStruct((s, w) if scatter else (rows, lines, s, w), f32)
        for (s, w), (scatter, _) in zip(pairs, plan)
    ]
    out_shape += [jax.ShapeDtypeStruct((dp_size,) + a.shape, f32) for a in fulls]
    out_shape += [jax.ShapeDtypeStruct(a.shape, f32) for a in shares]
    results = pl.pallas_call(
        functools.partial(exchange_kernel, (t_size, dp_size), plan, n_full, n_share),
        out_shape=out_shape,
        in_specs=[vmem] * len(parts) + [anywhere] * extra,
        out_specs=[vmem] * len(parts) + [anywhere] * extra,
        scratch_shapes=scratch,
        compiler_params=pltpu.CompilerParams(
            collective_id=number, has_side_effects=True, vmem_limit_bytes=32 << 20
        ),
        name=f"exchange_{number}",
    )(*[a.reshape(rows, lines, s, w) for (a, _, _), (s, w) in zip(parts, pairs)], *fulls, *shares)
    sums = [
        r if scatter else r.reshape(a.shape)
        for r, (a, scatter, _) in zip(results, parts)
    ]
    return sums, results[len(parts) : len(parts) + n_full], results[len(parts) + n_full :]


def softplus(v):
    return jnp.maximum(v, 0.0) + jnp.log1p(jnp.exp(-jnp.abs(v)))


def sigmoid(v):
    return 1.0 / (1.0 + jnp.exp(-v))


def scan_forward_kernel(
    keep, act, low, w_step, bias, alog, b, c, gate, skip, mixed, hist, pre, result, step, drive
):
    pre[...] = jnp.dot(low[...], w_step[...], preferred_element_type=jnp.float32) + bias[...]
    step[...] = softplus(pre[...])
    drive[...] = step[...] * act[...]
    rate = -jnp.exp(alog[...])

    def group(g, h):
        base = pl.multiple_of(g * GROUP, GROUP)
        steps = step[pl.ds(base, GROUP), :]
        drives = drive[pl.ds(base, GROUP), :]
        rows = []
        for j in range(GROUP):
            t = base + j
            decay = jnp.exp(steps[j : j + 1, :] * rate) * keep[t]
            b_wide = jnp.tile(b[t], (1, h.shape[1] // b.shape[2]))
            c_wide = jnp.tile(c[t], (1, h.shape[1] // c.shape[2]))
            h = decay * h + drives[j : j + 1, :] * b_wide
            hist[t] = h
            rows.append(jnp.sum(h * c_wide, axis=0, keepdims=True))
        result[pl.ds(base, GROUP), :] = jnp.concatenate(rows, axis=0)
        return h

    lax.fori_loop(0, act.shape[0] // GROUP, group, jnp.zeros(alog.shape, jnp.float32))
    result[...] = result[...] + skip[...] * act[...]
    z = gate[...]
    mixed[...] = (result[...] * (z * sigmoid(z))).astype(mixed.dtype)


def scan_forward(keep, act, low, w_step, bias, alog, b, c, gate, skip):
    n, width = act.shape
    f32 = jnp.float32
    vmem = pl.BlockSpec(memory_space=pltpu.VMEM)
    shapes = [
        jax.ShapeDtypeStruct((n, width), jnp.bfloat16),
        jax.ShapeDtypeStruct((n,) + alog.shape, f32),
        jax.ShapeDtypeStruct((n, width), f32),
        jax.ShapeDtypeStruct((n, width), f32),
    ]
    return pl.pallas_call(
        scan_forward_kernel,
        out_shape=shapes,
        in_specs=[pl.BlockSpec(memory_space=pltpu.SMEM)] + [vmem] * 9,
        out_specs=[vmem] * 4,
        scratch_shapes=[pltpu.VMEM((n, width), f32)] * 2,
        compiler_params=pltpu.CompilerParams(vmem_limit_bytes=40 << 20),
        name="scan_forward",
    )(keep, act, low, w_step, bias, alog, b, c, gate, skip)


def scan_backward_kernel(
    keep, d_mixed, act, alog, b, c, gate, skip, hist, pre, result, w_step,
    d_act, step_grad, d_low, d_b, d_c, d_gate, d_vec, d_alog,
    step, drive, d_y, sum_decay, sum_b,
):
    z = gate[...]
    sig = sigmoid(z)
    d_y[...] = d_mixed[...] * (z * sig)
    d_gate[...] = d_mixed[...] * result[...] * (sig * (1.0 + z * (1.0 - sig)))
    step[...] = softplus(pre[...])
    drive[...] = step[...] * act[...]
    rate = -jnp.exp(alog[...])
    n, width = act.shape
    lanes = b.shape[2]
    copies = width // lanes
    groups = n // GROUP

    def fold(v):
        total = v[:, :lanes]
        for k in range(1, copies):
            total = total + v[:, k * lanes : (k + 1) * lanes]
        return total

    def group(i, carry):
        later, alog_sum = carry
        base = pl.multiple_of((groups - 1 - i) * GROUP, GROUP)
        steps = step[pl.ds(base, GROUP), :]
        drives = drive[pl.ds(base, GROUP), :]
        d_ys = d_y[pl.ds(base, GROUP), :]
        rows_decay, rows_b = [None] * GROUP, [None] * GROUP
        for j in reversed(range(GROUP)):
            t = base + j
            step_t = steps[j : j + 1, :]
            d_y_t = d_ys[j : j + 1, :]
            b_wide = jnp.tile(b[t], (1, copies))
            c_wide = jnp.tile(c[t], (1, copies))
            decay = jnp.exp(step_t * rate) * keep[t]
            before = hist[jnp.maximum(t - 1, 0)]
            lam = d_y_t * c_wide + later
            through = lam * decay
            kept = through * before
            rows_decay[j] = jnp.sum(kept * rate, axis=0, keepdims=True)
            rows_b[j] = jnp.sum(lam * b_wide, axis=0, keepdims=True)
            alog_sum = alog_sum + kept * step_t
            d_b[t] = fold(lam * drives[j : j + 1, :])
            d_c[t] = fold(d_y_t * hist[t])
            later = through
        sum_decay[pl.ds(base, GROUP), :] = jnp.concatenate(rows_decay, axis=0)
        sum_b[pl.ds(base, GROUP), :] = jnp.concatenate(rows_b, axis=0)
        return later, alog_sum

    zero = jnp.zeros(alog.shape, jnp.float32)
    unused, alog_sum = lax.fori_loop(0, groups, group, (zero, zero))
    d_alog[...] = alog_sum * rate
    a = act[...].astype(jnp.float32)
    d_act[...] = sum_b[...] * step[...] + d_y[...] * skip[...]
    d_pre = (sum_decay[...] + sum_b[...] * a) * sigmoid(pre[...])
    step_grad[...] = d_pre.astype(step_grad.dtype)
    d_low[...] = lax.dot_general(
        step_grad[...], w_step[...], (((1,), (1,)), ((), ())), preferred_element_type=jnp.float32
    )
    d_vec[0:1, :] = jnp.sum(d_pre, axis=0, keepdims=True)
    d_vec[1:2, :] = jnp.sum(d_y[...] * a, axis=0, keepdims=True)


def scan_backward(keep, d_mixed, act, alog, b, c, gate, skip, hist, pre, result, w_step):
    n, width = act.shape
    f32 = jnp.float32
    vmem = pl.BlockSpec(memory_space=pltpu.VMEM)
    wide = jax.ShapeDtypeStruct((n, width), f32)
    shapes = [
        wide,
        jax.ShapeDtypeStruct((n, width), jnp.bfloat16),
        jax.ShapeDtypeStruct((n, w_step.shape[0]), f32),
        jax.ShapeDtypeStruct(b.shape, f32),
        jax.ShapeDtypeStruct(c.shape, f32),
        wide,
        jax.ShapeDtypeStruct((2, width), f32),
        jax.ShapeDtypeStruct(alog.shape, f32),
    ]
    return pl.pallas_call(
        scan_backward_kernel,
        out_shape=shapes,
        in_specs=[pl.BlockSpec(memory_space=pltpu.SMEM)] + [vmem] * 11,
        out_specs=[vmem] * 8,
        scratch_shapes=[pltpu.VMEM((n, width), f32)] * 5,
        compiler_params=pltpu.CompilerParams(vmem_limit_bytes=48 << 20),
        name="scan_backward",
    )(keep, d_mixed, act, alog, b, c, gate, skip, hist, pre, result, w_step)


def doc_masks(doc_ids, float_type):
    seq_len = doc_ids.shape[0]
    fresh = jnp.concatenate([jnp.ones((1,), jnp.bool_), doc_ids[1:] != doc_ids[:-1]])
    carry_mask = jnp.where(fresh, 0.0, 1.0).astype(float_type)
    places = jnp.arange(seq_len, dtype=jnp.int32)
    apart = places[:, None] - places[None, :]
    allowed = (apart >= 0) & (apart < WINDOW) & (doc_ids[:, None] == doc_ids[None, :])
    return (carry_mask, allowed)


def to_half(values):
    return values.astype(jnp.bfloat16)


def swiglu(gate_up):
    return jax.nn.silu(gate_up[:, 0]) * gate_up[:, 1]


def ffn_forward(resid, gain_vec, gate_up_weight, down_weight):
    normed_value, norm_back = jax.vjp(rms_norm, resid, gain_vec)
    normed = to_half(normed_value)
    gate_up = jnp.einsum("td,dsf->tsf", normed, gate_up_weight, preferred_element_type=jnp.float32)
    hidden_value, swiglu_back = jax.vjp(swiglu, gate_up)
    hidden = to_half(hidden_value)
    partial_out = jnp.dot(hidden, down_weight, preferred_element_type=jnp.float32)
    return (partial_out, (normed, hidden, norm_back, swiglu_back))


def ffn_backward(low_out, saved, gate_up_weight, down_weight):
    normed, hidden, norm_back, swiglu_back = saved
    d_hidden = jnp.einsum("td,fd->tf", low_out, down_weight, preferred_element_type=jnp.float32)
    (d_gate_value,) = swiglu_back(d_hidden)
    d_gate_up = to_half(d_gate_value)
    d_norm_part = jnp.einsum(
        "tsf,dsf->td", d_gate_up, gate_up_weight, preferred_element_type=jnp.float32
    )
    return (d_norm_part, d_gate_up)


def body(
    tokens,
    segments,
    cotangent,
    mixer_input_weight,
    conv_w,
    conv_b,
    w_state,
    w_step,
    dt_bias,
    a_log,
    d_skip,
    w_mix_out,
    w_gate_up_early,
    w_down_early,
    w_qkv,
    w_attn_out,
    w_gate_up,
    w_down,
    gain_one,
    gain_two,
    gain_three,
    gain_four,
):
    resid_in = tokens[0].astype(jnp.float32)
    doc_ids = segments[0]
    seq_len, model = resid_in.shape
    t_size, dp_size = lax.axis_size("tensor"), lax.axis_size("dp")
    share_rows = seq_len // t_size
    share_start = lax.axis_index("tensor") * share_rows
    low_rank = w_step.shape[0]
    channels, state_size = a_log.shape
    heads_here = w_attn_out.shape[0] // HEAD
    score_scale = HEAD ** (-0.5)
    carry_mask, allowed = doc_masks(doc_ids, jnp.float32)
    f32 = jnp.float32

    def conv_piece(conv_in, taps, shift_bias):
        return causal_conv(conv_in, doc_ids, taps, shift_bias)

    def by_owner(values):
        n, w = values.shape
        return jnp.swapaxes(values.astype(f32).reshape(n, dp_size, w // dp_size), 0, 1)

    def whole(gathered):
        return to_half(gathered.reshape((-1,) + gathered.shape[2:]))

    first_normalized_input = to_half(rms_norm(resid_in, gain_one))
    mixer_input_projected = jnp.einsum(
        "oc,cyb->oyb",
        first_normalized_input,
        mixer_input_weight,
        preferred_element_type=f32,
    )
    conv_in = mixer_input_projected[:, 0]
    gate_z = mixer_input_projected[:, 1]
    conv_value, conv_back = jax.vjp(conv_piece, conv_in, conv_w, conv_b)
    conv_act = to_half(conv_value)
    state_part = jnp.dot(conv_act, w_state, preferred_element_type=f32)
    (state_proj,), unused, (all_normed_one,) = exchange(
        1, [(state_part, False, 1)], [], [by_owner(first_normalized_input)]
    )
    step_low = to_half(state_proj[:, :low_rank])
    b_coef = state_proj[:, low_rank : low_rank + state_size]
    c_coef = state_proj[:, low_rank + state_size :]
    b_wide = jnp.broadcast_to(b_coef[:, :, None], (seq_len, state_size, 128))
    c_wide = jnp.broadcast_to(c_coef[:, :, None], (seq_len, state_size, 128))
    alog_rows = a_log.T
    mixer_out, hist, step_pre, scan_result = scan_forward(
        carry_mask, conv_act, step_low, w_step, dt_bias[None], alog_rows,
        b_wide, c_wide, gate_z, d_skip[None],
    )
    mixer_part = jnp.dot(mixer_out, w_mix_out, preferred_element_type=f32)
    grad_four = cotangent[0].astype(f32)
    (mixer_sum,), (all_low_four,), (all_mixer_out,) = exchange(
        2, [(mixer_part, False, 4)], [grad_four], [by_owner(mixer_out)]
    )
    resid_one = resid_in + mixer_sum
    early_part, early_saved = ffn_forward(resid_one, gain_two, w_gate_up_early, w_down_early)
    (early_sum,), unused, (all_normed_two, all_hidden_early) = exchange(
        3, [(early_part, False, 4)], [], [by_owner(early_saved[0]), by_owner(early_saved[1])]
    )
    resid_two = resid_one + early_sum
    norm_three, norm_three_back = jax.vjp(rms_norm, resid_two, gain_three)
    normed_three = to_half(norm_three)
    qkv_all = to_half(
        jnp.einsum("td,dsq->tsq", normed_three, w_qkv, preferred_element_type=f32)
    )
    queries = qkv_all[:, 0].reshape(seq_len, heads_here, HEAD)
    keys_all = qkv_all[:, 1].reshape(seq_len, heads_here, HEAD)
    values_all = qkv_all[:, 2].reshape(seq_len, heads_here, HEAD)
    raw_scores = (
        jnp.einsum("thd,shd->hts", queries, keys_all, preferred_element_type=f32)
        * score_scale
    )
    masked = jnp.where(allowed[None], raw_scores, -1000000000.0)
    softmax_out = jax.nn.softmax(masked, axis=-1)
    soft_low = to_half(softmax_out)
    attended = to_half(
        jnp.einsum("hts,shd->thd", soft_low, values_all, preferred_element_type=f32)
    ).reshape(seq_len, heads_here * HEAD)
    attn_part = jnp.dot(attended, w_attn_out, preferred_element_type=f32)
    (attn_sum,), unused, (all_normed_three, all_attended) = exchange(
        4, [(attn_part, False, 4)], [], [by_owner(normed_three), by_owner(attended)]
    )
    resid_three = resid_two + attn_sum
    late_part, late_saved = ffn_forward(resid_three, gain_four, w_gate_up, w_down)
    d_four_part, d_gate_up = ffn_backward(cotangent[0], late_saved, w_gate_up, w_down)
    (d_normed_four, late_share), (all_d_gate_up,), (all_normed_four, all_hidden) = exchange(
        5,
        [(d_four_part, False, 4), (late_part, True, 2)],
        [d_gate_up.astype(f32).reshape(seq_len, -1)],
        [by_owner(late_saved[0]), by_owner(late_saved[1])],
    )
    mixed = to_half(lax.dynamic_slice_in_dim(resid_three, share_start, share_rows, 0) + late_share)[
        None
    ]
    back_three, grad_gain_four = late_saved[2](d_normed_four)
    grad_resid_three = grad_four + back_three
    low_three = to_half(grad_resid_three)
    d_attended = to_half(
        jnp.einsum("td,qd->tq", low_three, w_attn_out, preferred_element_type=f32)
    ).reshape(seq_len, heads_here, HEAD)
    d_soft = jnp.einsum("thd,shd->hts", d_attended, values_all, preferred_element_type=f32)
    d_values = jnp.einsum("hts,thd->shd", soft_low, d_attended, preferred_element_type=f32)
    delta = jnp.sum(softmax_out * d_soft, axis=-1, keepdims=True)
    d_scores = to_half(softmax_out * (d_soft - delta))
    d_queries = (
        jnp.einsum("hts,shd->thd", d_scores, keys_all, preferred_element_type=f32)
        * score_scale
    )
    d_keys = (
        jnp.einsum("hts,thd->shd", d_scores, queries, preferred_element_type=f32)
        * score_scale
    )
    d_qkv = to_half(
        jnp.stack([d_queries, d_keys, d_values], axis=1).reshape(seq_len, 3, heads_here * HEAD)
    )
    d_three_part = jnp.einsum("tsq,dsq->td", d_qkv, w_qkv, preferred_element_type=f32)
    (d_normed_three,), (all_low_three, all_d_qkv), (all_gain_four,) = exchange(
        6,
        [(d_three_part, False, 4)],
        [low_three.astype(f32), d_qkv.astype(f32).reshape(seq_len, -1)],
        [by_owner(grad_gain_four[None])],
    )
    back_two, grad_gain_three = norm_three_back(d_normed_three)
    grad_resid_two = grad_resid_three + back_two
    low_two = to_half(grad_resid_two)
    d_two_part, d_gate_up_early = ffn_backward(
        low_two, early_saved, w_gate_up_early, w_down_early
    )
    (d_normed_two,), (all_low_two, all_d_gate_up_early), (all_gain_three,) = exchange(
        7,
        [(d_two_part, False, 4)],
        [low_two.astype(f32), d_gate_up_early.astype(f32).reshape(seq_len, -1)],
        [by_owner(grad_gain_three[None])],
    )
    back_one, grad_gain_two = early_saved[2](d_normed_two)
    grad_resid_one = grad_resid_two + back_one
    low_one = to_half(grad_resid_one)
    d_mixer_out = jnp.einsum("td,ed->te", low_one, w_mix_out, preferred_element_type=f32)
    d_conv_scan, step_grad, d_step_low, d_b_wide, d_c_wide, d_gate_z, d_vec, d_alog_rows = (
        scan_backward(
            carry_mask, d_mixer_out, conv_act, alog_rows, b_wide, c_wide, gate_z, d_skip[None],
            hist, step_pre, scan_result, w_step,
        )
    )
    grad_step = jnp.einsum("tr,te->re", step_low, step_grad, preferred_element_type=f32)
    d_state_part = jnp.concatenate(
        [d_step_low, jnp.sum(d_b_wide, axis=-1), jnp.sum(d_c_wide, axis=-1)], axis=1
    )
    (d_state_proj,), (all_low_one,), (all_gain_two, all_step) = exchange(
        8,
        [(d_state_part, False, 1)],
        [low_one.astype(f32)],
        [by_owner(grad_gain_two[None]), grad_step.reshape(dp_size, low_rank // dp_size, channels)],
    )
    conv_single = conv_act.astype(f32)
    grad_state = jnp.einsum(
        "te,tk->ek",
        conv_single,
        d_state_proj,
        precision=EXACT_MATMUL,
        preferred_element_type=f32,
    )
    d_conv_act = d_conv_scan + jnp.einsum(
        "tk,ek->te",
        d_state_proj,
        w_state.astype(f32),
        precision=EXACT_MATMUL,
        preferred_element_type=f32,
    )
    d_conv_in, grad_conv_w, grad_conv_b = conv_back(d_conv_act)
    mixer_input_gradient = to_half(jnp.stack([d_conv_in, d_gate_z], axis=1))
    first_branch_gradient = jnp.einsum(
        "jcz,ycz->jy", mixer_input_gradient, mixer_input_weight, preferred_element_type=f32
    )
    small_rows = jnp.concatenate(
        [d_alog_rows, grad_conv_w.T, grad_conv_b[None], d_vec], axis=0
    )
    (d_normed_one,), (all_d_mix,), (all_state, all_small) = exchange(
        9,
        [(first_branch_gradient, True, 2)],
        [mixer_input_gradient.astype(f32).reshape(seq_len, -1)],
        [grad_state.reshape(dp_size, channels // dp_size, -1), by_owner(small_rows)],
    )
    resid_share = lax.dynamic_slice_in_dim(resid_in, share_start, share_rows, 0)
    unused_norm, share_norm_back = jax.vjp(rms_norm, resid_share, gain_one)
    back_in, gain_one_part = share_norm_back(d_normed_one)
    tokens_grad = to_half(
        lax.dynamic_slice_in_dim(grad_resid_one, share_start, share_rows, 0) + back_in
    )[None]
    whole_gain_one = lax.psum(gain_one_part, ("dp", "tensor"))

    def grad_of(left, right, parts=1):
        result = jnp.dot(whole(left).T, whole(right), preferred_element_type=f32)
        if parts > 1:
            result = result.reshape(result.shape[0], parts, -1)
        return result

    small = jnp.sum(all_small, axis=0)
    taps = conv_w.shape[1]
    at = state_size + taps
    return (
        mixed,
        tokens_grad,
        grad_of(all_normed_one, all_d_mix, 2),
        small[state_size:at].T,
        small[at],
        jnp.sum(all_state, axis=0),
        jnp.sum(all_step, axis=0),
        small[at + 1],
        small[:state_size].T,
        small[at + 2],
        grad_of(all_mixer_out, all_low_one),
        grad_of(all_normed_two, all_d_gate_up_early, 2),
        grad_of(all_hidden_early, all_low_two),
        grad_of(all_normed_three, all_d_qkv, 3),
        grad_of(all_attended, all_low_three),
        grad_of(all_normed_four, all_d_gate_up, 2),
        grad_of(all_hidden, all_low_four),
        whole_gain_one,
        jnp.sum(all_gain_two, axis=0)[0],
        jnp.sum(all_gain_three, axis=0)[0],
        jnp.sum(all_gain_four, axis=0)[0],
    )


def solution(mesh):
    in_specs = (
        P("dp", None, None),
        P("dp", None),
        P("dp", None, None),
        P(None, None, "tensor"),
        P("tensor", None),
        P("tensor"),
        P("tensor", None),
        P(None, "tensor"),
        P("tensor"),
        P("tensor", None),
        P("tensor"),
        P("tensor", None),
        P(None, None, "tensor"),
        P("tensor", None),
        P(None, None, "tensor"),
        P("tensor", None),
        P(None, None, "tensor"),
        P("tensor", None),
        P(),
        P(),
        P(),
        P(),
    )
    out_specs = (
        P("dp", "tensor", None),
        P("dp", "tensor", None),
        P("dp", None, "tensor"),
        P(("tensor", "dp"), None),
        P(("tensor", "dp")),
        P(("tensor", "dp"), None),
        P("dp", "tensor"),
        P(("tensor", "dp")),
        P(("tensor", "dp"), None),
        P(("tensor", "dp")),
        P(("tensor", "dp"), None),
        P("dp", None, "tensor"),
        P(("tensor", "dp"), None),
        P("dp", None, "tensor"),
        P(("tensor", "dp"), None),
        P("dp", None, "tensor"),
        P(("tensor", "dp"), None),
        P(),
        P("dp"),
        P("dp"),
        P("dp"),
    )
    return jax.shard_map(body, mesh=mesh, in_specs=in_specs, out_specs=out_specs, check_vma=False)
```
